32 devices in a mesh: rep: 4 (over y, x), fsdp: 8 (over z, core).
Axes of the slice: x: 2, y: 2, z: 4, core: 2. Of those that a mesh axis runs over, the one named last changes fastest.
Arguments:
- hidden_acts: bfloat16 [4, 4096, 256], P('rep', 'fsdp'), may hold values from -6 to 6
- out_grads: bfloat16 [4, 4096, 8192], P('rep', 'fsdp'), may hold values from -0.25 to 0.25
- anchor: float32 [256, 8192], P('fsdp'), may hold values from -6 to 6
- drift: float32 [4, 256, 8192], P('rep', 'fsdp'), may hold values from -120 to 120, as said below
- adam_first: float32 [4, 256, 8192], P('rep', 'fsdp'), may hold values from -6 to 6
- adam_second: float32 [4, 256, 8192], P('rep', 'fsdp'), may hold values from 0.3 to 3
- outer_momentum: float32 [256, 8192], P('fsdp'), may hold values from -6 to 6
Outputs:
- new_first: float32 [4, 256, 8192], P('rep', 'fsdp')
- new_second: float32 [4, 256, 8192], P('rep', 'fsdp')
- new_momentum: float32 [256, 8192], P('fsdp')
- new_anchor: float32 [256, 8192], P('fsdp')
The draws below stay inside these ranges and needn't reach their ends.
Inputs may be any that keep to these rules, and one draw needn't show every extreme that they name: drift entries are finite reals.
All inputs are finite; a program needn't handle non-finite values.
Results may differ from the reference program's by a relative error of at most 0.0003.
Values sent between devices are 32-bit elements; how exact they have to be, the bound alone decides.
A program may use at most 128 MiB of HBM per device.

```python
import math
import jax
import jax.numpy as jnp
from jax import lax

D = 8192
TOK_DEV = 512
INNER_STEP = 100
ROWS = 256
TOKENS = 4096
REPLICAS = 4


def draw_drift(key, part):
    pieces = jax.random.split(key, 3)
    position = jnp.arange(ROWS, dtype=jnp.float32) / max(ROWS - 1, 1)
    row_scale = jnp.exp(position * math.log(3.0)) * jnp.exp(jax.random.uniform(pieces[1], (ROWS,), jnp.float32, 0.0, math.log(3.3)))
    col_scale = jnp.exp(jax.random.uniform(pieces[2], (D,), jnp.float32, 0.0, math.log(3.3)))
    base = jnp.clip(jax.random.normal(pieces[0], (REPLICAS, ROWS, D), jnp.float32), -6.0, 6.0)
    return (0.6 * base * row_scale[None, :, None] * col_scale[None, None, :]).astype(jnp.float32)


def spiked(values, stream_key, source, target, parts, factor):
    owner, partner = [(jnp.arange(values.shape[axis_at]) // (values.shape[axis_at] // parts)).reshape([-1 if axis == axis_at else 1 for axis in range(values.ndim)]) for axis_at in (source, target)]
    chosen = jax.random.permutation(stream_key, parts)[partner]
    strong = (owner == chosen) | (owner == (partner + parts // 2) % parts)
    return jnp.where(strong, factor * values, values)


def levels(own_key, shape, cuts, smallest, high):
    loudness = 1.0
    for axis_at, blocks in cuts:
        steps = jax.random.uniform(jax.random.fold_in(jax.random.fold_in(own_key, 6), axis_at), (blocks,), jnp.float32, smallest / len(cuts), high / len(cuts))
        loudness = loudness * jnp.repeat(jnp.exp(steps), shape[axis_at] // blocks).reshape((-1,) + (1,) * (len(shape) - 1 - axis_at))
    return loudness


def bell_draw(key, extent, scale, bound, cuts=(), kind=jnp.bfloat16):
    loudness = levels(key, extent, cuts, -0.22, 0.18) if cuts else 1.0
    drawn = jax.random.normal(key, extent, jnp.float32) * scale * loudness
    return jnp.minimum(jnp.maximum(drawn, -bound), bound).astype(kind)


def noise_with(key, dims, deviation, reach, cuts, heavy, kind=jnp.bfloat16):
    result = deviation * jax.random.normal(key, dims, jnp.float32)
    if cuts:
        result = result * levels(key, dims, cuts, -0.22, 0.18)
    return jnp.clip(spiked(result, jax.random.fold_in(key, 3), *heavy), -reach, reach).astype(kind)


def setup_inputs(seed: int = 0) -> dict:
    keys = jax.random.split(jax.random.key(seed), 8)
    return {
        "hidden_acts": noise_with(keys[0], (REPLICAS, TOKENS, ROWS), 1.0, 6.0, ((0, 4), (1, 8)), (1, 2, 8, 2.0)),
        "out_grads": bell_draw(keys[1], (REPLICAS, TOKENS, D), (TOKENS ** -0.5), 0.25, ((0, 4), (1, 8))),
        "anchor": bell_draw(keys[2], (ROWS, D), 1.0, 6.0, ((0, 8),), jnp.float32),
        "drift": draw_drift(jax.random.fold_in(keys[7], 71), 0),
        "adam_first": bell_draw(keys[4], (REPLICAS, ROWS, D), 1.0, 6.0, ((0, 4), (1, 8)), jnp.float32),
        "adam_second": jnp.clip(jnp.exp(math.log(3.0) - 2.3025851 * jax.random.uniform(keys[5], (REPLICAS, ROWS, D), jnp.float32) ** levels(keys[5], (REPLICAS, ROWS, D), ((0, 4), (1, 8)), -0.2, 0.2)), 0.3, 3.0),
        "outer_momentum": bell_draw(keys[6], (ROWS, D), 0.5, 6.0, ((0, 8),), jnp.float32),
    }


beta_first = 0.9
beta_second = 0.95
inner_rate = 0.5
decay_weight = 0.1
outer_rate = 0.7
momentum_coef = 0.9

def replica_gradient(activations, cotangent):
    groups = TOKENS // TOK_DEV
    act_groups = activations.reshape(groups, TOK_DEV, ROWS)
    cot_groups = cotangent.reshape(groups, TOK_DEV, D)

    def accumulate(running, paired):
        partial_sum = jnp.dot(paired[0].T, paired[1], preferred_element_type=jnp.float32)
        return (running + partial_sum, None)
    summed, unused = lax.scan(accumulate, jnp.zeros((ROWS, D), jnp.float32), (act_groups, cot_groups))
    return summed

def reference(hidden_acts, out_grads, anchor, drift, adam_first, adam_second, outer_momentum):
    correction_one = 1.0 - beta_first ** INNER_STEP
    correction_two = 1.0 - beta_second ** INNER_STEP

    def per_replica(running, inputs):
        activations, cotangent, own_drift, first_old, second_old = inputs
        gradient = replica_gradient(activations, cotangent)
        moment_one = beta_first * first_old + (1.0 - beta_first) * gradient
        moment_two = beta_second * second_old + (1.0 - beta_second) * gradient * gradient
        update = moment_one / correction_one / (jnp.sqrt(moment_two / correction_two) + 1e-08) + decay_weight * (anchor + own_drift)
        pseudo = inner_rate * update - own_drift
        return (running + pseudo, (moment_one, moment_two))
    summed, moments = lax.scan(per_replica, jnp.zeros((ROWS, D), jnp.float32), (hidden_acts, out_grads, drift, adam_first, adam_second))
    new_first, new_second = moments
    average = summed / REPLICAS
    squares = jnp.sum(average * average)
    ceiling = 0.3 * math.sqrt(ROWS * D)
    factor = ceiling / jnp.maximum(jnp.sqrt(squares), ceiling)
    new_momentum = momentum_coef * outer_momentum + factor * average
    new_anchor = anchor - outer_rate * (factor * average + momentum_coef * new_momentum)
    return (new_first, new_second, new_momentum, new_anchor)
```

```python
import functools
import math

import jax
import jax.numpy as jnp
from jax import lax
from jax.experimental import pallas as pl
from jax.experimental.pallas import tpu as pltpu
from jax.sharding import PartitionSpec as P

INNER_STEP = 100
CORES = 2
CHUNKS = 16

beta_first = 0.9
beta_second = 0.95
inner_rate = 0.5
decay_weight = 0.1
outer_rate = 0.7
momentum_coef = 0.9
correction_one = 1.0 - beta_first**INNER_STEP
correction_two = 1.0 - beta_second**INNER_STEP

MESH = pl.DeviceIdType.MESH
ANCHOR, DRIFT, FIRST, SECOND, MOMENTUM = range(5)


def kernel(
    replicas, shards,
    acts_hbm, grads_hbm, anchor_hbm, drift_hbm, first_hbm, second_hbm, momentum_hbm,
    out_first, out_second, out_momentum, out_anchor,
    acts, acts_t, grads, part, swapped, chain, params, doubled, squares,
    acts_sem, grads_sem, params_sem, out_sem,
    swap_send, swap_recv, chain_send, chain_recv, double_send, double_recv,
    square_send, square_recv,
):
    chunks, _, width = grads.shape
    rows = params.shape[2]
    levels = shards // CORES
    stages = doubled.shape[0]
    rep = lax.axis_index("rep")
    shard = lax.axis_index("fsdp")
    z = shard // CORES
    core = shard % CORES
    other = 1 - core
    twin = (rep, z * CORES + other)
    above = (rep, lax.rem(shard + CORES, shards))
    below = (rep, lax.rem(shard + shards - CORES, shards))
    partners = []
    for stage in range(stages):
        bit = 2**stage
        partners.append(rep + bit - 2 * bit * ((rep // bit) % 2))

    barrier = pltpu.get_barrier_semaphore()

    @pl.loop(1, shards)
    def _(step):
        pl.semaphore_signal(
            barrier, inc=1, device_id=(rep, lax.rem(shard + step, shards)), device_id_type=MESH
        )

    for partner in partners:
        pl.semaphore_signal(barrier, inc=1, device_id=(partner, shard), device_id_type=MESH)

    def columns(k):
        return pl.ds(pl.multiple_of(k * width, width), width)

    def load_acts():
        return pltpu.make_async_copy(acts_hbm.at[0], acts, acts_sem)

    def load_grads(k):
        return pltpu.make_async_copy(
            grads_hbm.at[0, :, columns(k)], grads.at[k], grads_sem.at[k]
        )

    def load_param(which, k):
        source = (
            anchor_hbm, drift_hbm.at[0], first_hbm.at[0], second_hbm.at[0], momentum_hbm
        )[which]
        return pltpu.make_async_copy(
            source.at[:, columns(k)], params.at[which, k], params_sem.at[which, k]
        )

    def store_out(which, k):
        target = {
            FIRST: out_first.at[0], SECOND: out_second.at[0],
            MOMENTUM: out_momentum, ANCHOR: out_anchor,
        }[which]
        return pltpu.make_async_copy(
            params.at[which, k], target.at[:, columns(k)], out_sem.at[which, k]
        )

    load_acts().start()

    @pl.loop(0, chunks)
    def _(k):
        load_grads(k).start()

    @pl.loop(0, chunks)
    def _(k):
        for which in range(5):
            load_param(which, k).start()

    load_acts().wait()
    acts_t[...] = acts[...].T
    squares[shard] = jnp.zeros((8, 128), jnp.float32)
    pl.semaphore_wait(barrier, shards - 1 + stages)

    def swap(k):
        return pltpu.make_async_remote_copy(
            src_ref=part.at[k, other], dst_ref=swapped.at[k],
            send_sem=swap_send.at[k], recv_sem=swap_recv.at[k],
            device_id=twin, device_id_type=MESH,
        )

    def hop(k, dest, slot, target):
        return pltpu.make_async_remote_copy(
            src_ref=part.at[k, core, dest], dst_ref=chain.at[k, slot],
            send_sem=chain_send.at[k, dest], recv_sem=chain_recv.at[k, slot],
            device_id=target, device_id_type=MESH,
        )

    def double(stage, k):
        turn = lax.rem(k + stage, stages)
        partner = partners[0]
        for j in range(1, stages):
            partner = jnp.where(turn == j, partners[j], partner)
        source = params.at[DRIFT, k] if stage == 0 else doubled.at[stage - 1, k]
        return pltpu.make_async_remote_copy(
            src_ref=source, dst_ref=doubled.at[stage, k],
            send_sem=double_send.at[stage, k], recv_sem=double_recv.at[stage, k],
            device_id=(partner, shard), device_id_type=MESH,
        )

    def inside(k):
        return (k >= 0) & (k < chunks)

    def product(k):
        load_grads(k).wait()
        for at in range(0, width, 256):
            block = jnp.dot(
                acts_t[...], grads[k, :, at : at + 256], preferred_element_type=jnp.float32
            )
            for j in range(shards):
                part[k, j % CORES, j // CORES, :, at : at + 256] = block[j * rows : (j + 1) * rows]
        swap(k).start()

    def join(k):
        swap(k).wait_recv()
        part[k, core] += swapped[k]

    def add_hop(k, dest):
        hop(k, dest, dest, above).wait_recv()
        part[k, core, dest] += chain[k, dest]

    def send_up(k):
        for dest in range(levels - 1, 0, -1):
            @pl.when(dest > z)
            def _():
                @pl.when(z > 0)
                def _():
                    add_hop(k, dest)

                hop(k, dest, dest, above).start()

    def send_down(k):
        for dest in range(levels - 1):
            @pl.when(dest < z)
            def _():
                @pl.when(z < levels - 1)
                def _():
                    add_hop(k, dest)

                hop(k, dest, jnp.where(dest == z - 1, levels, dest), below).start()

    def inner_step(k):
        @pl.when(z > 0)
        def _():
            hop(k, z, z, above).wait_recv()
            part[k, core, z] += chain[k, z]

        @pl.when(z < levels - 1)
        def _():
            hop(k, z, levels, above).wait_recv()
            part[k, core, z] += chain[k, levels]

        for which in range(4):
            load_param(which, k).wait()
        gradient = part[k, core, z]
        drift = params[DRIFT, k]
        moment_one = beta_first * params[FIRST, k] + (1.0 - beta_first) * gradient
        moment_two = beta_second * params[SECOND, k] + (1.0 - beta_second) * gradient * gradient
        update = moment_one / correction_one / (
            jnp.sqrt(moment_two / correction_two) + 1e-08
        ) + decay_weight * (params[ANCHOR, k] + drift)
        params[FIRST, k] = moment_one
        params[SECOND, k] = moment_two
        params[DRIFT, k] = inner_rate * update - drift
        double(0, k).start()
        store_out(FIRST, k).start()
        store_out(SECOND, k).start()

    def add_replica(stage, k):
        double(stage, k).wait_recv()
        mine = params[DRIFT, k] if stage == 0 else doubled[stage - 1, k]
        total = mine + doubled[stage, k]
        if stage < stages - 1:
            doubled[stage, k] = total
            double(stage + 1, k).start()
        else:
            average = total / replicas
            doubled[stage, k] = average
            square = average * average
            folded = jnp.zeros((8, 128), jnp.float32)
            for i in range(0, rows, 8):
                for j in range(0, width, 128):
                    folded += square[i : i + 8, j : j + 128]
            squares[shard] += folded

    depth = jnp.maximum(z, levels - 1 - z)

    @pl.loop(0, chunks + 1 + levels + stages)
    def _(tick):
        @pl.when(inside(tick))
        def _():
            product(tick)

        @pl.when(inside(tick - 1))
        def _():
            join(tick - 1)

        up = tick - 1 - z

        @pl.when(inside(up))
        def _():
            send_up(up)

        down = tick - 1 - (levels - 1 - z)

        @pl.when(inside(down))
        def _():
            send_down(down)

        for stage in range(stages - 1, -1, -1):
            now = tick - 2 - depth - stage

            @pl.when(inside(now))
            def _():
                add_replica(stage, now)

        own = tick - 1 - depth

        @pl.when(inside(own))
        def _():
            inner_step(own)

    def tell(owner, target):
        return pltpu.make_async_remote_copy(
            src_ref=squares.at[owner], dst_ref=squares.at[owner],
            send_sem=square_send.at[target], recv_sem=square_recv.at[owner],
            device_id=(rep, target), device_id_type=MESH,
        )

    @pl.loop(1, shards)
    def _(step):
        tell(shard, lax.rem(shard + step, shards)).start()

    @pl.loop(0, chunks)
    def _(k):
        swap(k).wait_send()
        for dest in range(levels):
            @pl.when(dest != z)
            def _():
                hop(k, dest, dest, above).wait_send()

        for stage in range(stages):
            double(stage, k).wait_send()
        load_param(MOMENTUM, k).wait()
        store_out(FIRST, k).wait()
        store_out(SECOND, k).wait()

    @pl.loop(1, shards)
    def _(step):
        tell(lax.rem(shard + step, shards), lax.rem(shard + step, shards)).wait_recv()

    total = squares[0]
    for owner in range(1, shards):
        total += squares[owner]
    norm = jnp.sqrt(jnp.sum(total, keepdims=True))
    ceiling = 0.3 * math.sqrt(rows * shards * chunks * width)
    factor = ceiling / jnp.maximum(norm, ceiling)

    @pl.loop(0, chunks)
    def _(k):
        scaled = factor * doubled[stages - 1, k]
        momentum = momentum_coef * params[MOMENTUM, k] + scaled
        params[MOMENTUM, k] = momentum
        params[ANCHOR, k] = params[ANCHOR, k] - outer_rate * (scaled + momentum_coef * momentum)
        store_out(MOMENTUM, k).start()
        store_out(ANCHOR, k).start()

    @pl.loop(0, chunks)
    def _(k):
        store_out(MOMENTUM, k).wait()
        store_out(ANCHOR, k).wait()

    @pl.loop(1, shards)
    def _(step):
        tell(shard, lax.rem(shard + step, shards)).wait_send()


def per_device(replicas, shards, *args):
    acts, grads, anchor = args[:3]
    tokens, features = acts.shape[1:]
    rows, width = anchor.shape[0], anchor.shape[1] // CHUNKS
    levels = shards // CORES
    stages = replicas.bit_length() - 1
    f32 = jnp.float32
    dma = pltpu.SemaphoreType.DMA
    scratch = [
        pltpu.VMEM((tokens, features), acts.dtype),
        pltpu.VMEM((features, tokens), acts.dtype),
        pltpu.VMEM((CHUNKS, tokens, width), grads.dtype),
        pltpu.VMEM((CHUNKS, CORES, levels, rows, width), f32),
        pltpu.VMEM((CHUNKS, levels, rows, width), f32),
        pltpu.VMEM((CHUNKS, levels + 1, rows, width), f32),
        pltpu.VMEM((5, CHUNKS, rows, width), f32),
        pltpu.VMEM((stages, CHUNKS, rows, width), f32),
        pltpu.VMEM((shards, 8, 128), f32),
        dma, dma((CHUNKS,)), dma((5, CHUNKS)), dma((5, CHUNKS)),
        dma((CHUNKS,)), dma((CHUNKS,)),
        dma((CHUNKS, levels)), dma((CHUNKS, levels + 1)),
        dma((stages, CHUNKS)), dma((stages, CHUNKS)),
        dma((shards,)), dma((shards,)),
    ]
    moment = jax.ShapeDtypeStruct((1,) + anchor.shape, f32)
    outer = jax.ShapeDtypeStruct(anchor.shape, f32)
    anywhere = pl.BlockSpec(memory_space=pl.ANY)
    return pl.pallas_call(
        functools.partial(kernel, replicas, shards),
        out_shape=(moment, moment, outer, outer),
        in_specs=[anywhere] * 7,
        out_specs=(anywhere,) * 4,
        scratch_shapes=scratch,
        compiler_params=pltpu.CompilerParams(
            collective_id=0, has_side_effects=True, vmem_limit_bytes=60 * 2**20
        ),
        cost_estimate=pl.CostEstimate(
            flops=2 * tokens * features * anchor.shape[1],
            bytes_accessed=2 * tokens * anchor.shape[1] + 9 * 4 * anchor.size,
            transcendentals=anchor.size,
        ),
        name="outer_step",
    )(*args)


def solution(mesh):
    shared = P("fsdp", None)
    own = P("rep", "fsdp", None)
    return jax.shard_map(
        functools.partial(per_device, mesh.shape["rep"], mesh.shape["fsdp"]),
        mesh=mesh,
        in_specs=(own, own, shared, own, own, own, shared),
        out_specs=(own, own, shared, shared),
        check_vma=False,
    )
```

```python
import functools
import math

import jax
import jax.numpy as jnp
from jax import lax
from jax.experimental import pallas as pl
from jax.experimental.pallas import tpu as pltpu
from jax.sharding import PartitionSpec as P

INNER_STEP = 100
CORES = 2
CHUNKS = 16

beta_first = 0.9
beta_second = 0.95
inner_rate = 0.5
decay_weight = 0.1
outer_rate = 0.7
momentum_coef = 0.9
correction_one = 1.0 - beta_first**INNER_STEP
correction_two = 1.0 - beta_second**INNER_STEP

MESH = pl.DeviceIdType.MESH
ANCHOR, DRIFT, FIRST, SECOND, MOMENTUM = range(5)
AHEAD = 4
SLACK = 2


def kernel(
    replicas, shards,
    acts_hbm, grads_hbm, anchor_hbm, drift_hbm, first_hbm, second_hbm, momentum_hbm,
    out_first, out_second, out_momentum, out_anchor,
    acts, acts_t, grads, part, swapped, chain, pseudo, doubled, squares,
    acts_sem, grads_sem, params_sem,
    swap_send, swap_recv, chain_send, chain_recv, double_send, double_recv,
    square_send, square_recv,
):
    chunks, _, width = grads.shape
    rows = pseudo.shape[1]
    levels = shards // CORES
    stages = doubled.shape[0]
    rep = lax.axis_index("rep")
    shard = lax.axis_index("fsdp")
    z = shard // CORES
    core = shard % CORES
    other = 1 - core
    twin = (rep, z * CORES + other)
    above = (rep, lax.rem(shard + CORES, shards))
    below = (rep, lax.rem(shard + shards - CORES, shards))
    partners = []
    for stage in range(stages):
        bit = 2**stage
        partners.append(rep + bit - 2 * bit * ((rep // bit) % 2))

    barrier = pltpu.get_barrier_semaphore()

    @pl.loop(1, shards)
    def _(step):
        pl.semaphore_signal(
            barrier, inc=1, device_id=(rep, lax.rem(shard + step, shards)), device_id_type=MESH
        )

    for partner in partners:
        pl.semaphore_signal(barrier, inc=1, device_id=(partner, shard), device_id_type=MESH)

    def columns(k):
        return pl.ds(pl.multiple_of(k * width, width), width)

    def load_acts():
        return pltpu.make_async_copy(acts_hbm.at[0], acts, acts_sem)

    def load_grads(k):
        return pltpu.make_async_copy(
            grads_hbm.at[0, :, columns(k)], grads.at[k], grads_sem.at[k]
        )

    def load_param(which, k):
        source, target = (
            (anchor_hbm, out_anchor),
            (drift_hbm.at[0], None),
            (first_hbm.at[0], out_first.at[0]),
            (second_hbm.at[0], out_second.at[0]),
            (momentum_hbm, out_momentum),
        )[which]
        return pltpu.make_async_copy(
            source.at[:, columns(k)],
            pseudo.at[k] if which == DRIFT else target.at[:, columns(k)],
            params_sem.at[which, k],
        )

    load_acts().start()

    for k in range(AHEAD):
        load_grads(k).start()

    load_acts().wait()
    acts_t[...] = acts[...].T
    squares[shard] = jnp.zeros((8, 128), jnp.float32)
    pl.semaphore_wait(barrier, shards - 1 + stages)

    def swap(k):
        return pltpu.make_async_remote_copy(
            src_ref=part.at[k, other], dst_ref=swapped.at[k],
            send_sem=swap_send.at[k], recv_sem=swap_recv.at[k],
            device_id=twin, device_id_type=MESH,
        )

    def hop(k, dest, slot, target):
        return pltpu.make_async_remote_copy(
            src_ref=part.at[k, core, dest], dst_ref=chain.at[k, slot],
            send_sem=chain_send.at[k, dest], recv_sem=chain_recv.at[k, slot],
            device_id=target, device_id_type=MESH,
        )

    def double(stage, k):
        turn = lax.rem(k + stage, stages)
        partner = partners[0]
        for j in range(1, stages):
            partner = jnp.where(turn == j, partners[j], partner)
        source = pseudo.at[k] if stage == 0 else doubled.at[stage - 1, k]
        return pltpu.make_async_remote_copy(
            src_ref=source, dst_ref=doubled.at[stage, k],
            send_sem=double_send.at[stage, k], recv_sem=double_recv.at[stage, k],
            device_id=(partner, shard), device_id_type=MESH,
        )

    def inside(k):
        return (k >= 0) & (k < chunks)

    def product(k):
        load_grads(k).wait()

        @pl.when(k + AHEAD < chunks)
        def _():
            load_grads(k + AHEAD).start()

        for which in range(5):
            load_param(which, k).start()

        for at in range(0, width, 256):
            block = jnp.dot(
                acts_t[...], grads[k, :, at : at + 256], preferred_element_type=jnp.float32
            )
            for j in range(shards):
                part[k, j % CORES, j // CORES, :, at : at + 256] = block[j * rows : (j + 1) * rows]
        swap(k).start()

    def join(k):
        swap(k).wait_recv()
        part[k, core] += swapped[k]

    def add_hop(k, dest):
        hop(k, dest, dest, above).wait_recv()
        part[k, core, dest] += chain[k, dest]

    def send_up(k):
        for dest in range(levels - 1, 0, -1):
            @pl.when(dest > z)
            def _():
                @pl.when(z > 0)
                def _():
                    add_hop(k, dest)

                hop(k, dest, dest, above).start()

    def send_down(k):
        for dest in range(levels - 1):
            @pl.when(dest < z)
            def _():
                @pl.when(z < levels - 1)
                def _():
                    add_hop(k, dest)

                hop(k, dest, jnp.where(dest == z - 1, levels, dest), below).start()

    def inner_step(k):
        @pl.when(z > 0)
        def _():
            hop(k, z, z, above).wait_recv()
            part[k, core, z] += chain[k, z]

        @pl.when(z < levels - 1)
        def _():
            hop(k, z, levels, above).wait_recv()
            part[k, core, z] += chain[k, levels]

        for which in range(4):
            load_param(which, k).wait()
        here = columns(k)
        gradient = part[k, core, z]
        drift = pseudo[k]
        moment_one = beta_first * out_first[0, :, here] + (1.0 - beta_first) * gradient
        moment_two = beta_second * out_second[0, :, here] + (1.0 - beta_second) * gradient * gradient
        update = moment_one / correction_one / (
            jnp.sqrt(moment_two / correction_two) + 1e-08
        ) + decay_weight * (out_anchor[:, here] + drift)
        pseudo[k] = inner_rate * update - drift
        double(0, k).start()
        out_first[0, :, here] = moment_one
        out_second[0, :, here] = moment_two

    def add_replica(stage, k):
        double(stage, k).wait_recv()
        mine = pseudo[k] if stage == 0 else doubled[stage - 1, k]
        total = mine + doubled[stage, k]
        if stage < stages - 1:
            doubled[stage, k] = total
            double(stage + 1, k).start()
        else:
            average = total / replicas
            doubled[stage, k] = average
            square = average * average
            folded = jnp.zeros((8, 128), jnp.float32)
            for i in range(0, rows, 8):
                for j in range(0, width, 128):
                    folded += square[i : i + 8, j : j + 128]
            squares[shard] += folded

    depth = SLACK * jnp.maximum(z, levels - 1 - z)

    @pl.loop(0, chunks + 2 + SLACK * (levels - 1) + stages)
    def _(tick):
        @pl.when(inside(tick))
        def _():
            product(tick)

        @pl.when(inside(tick - 1))
        def _():
            join(tick - 1)

        up = tick - 1 - SLACK * z

        @pl.when(inside(up))
        def _():
            send_up(up)

        down = tick - 1 - SLACK * (levels - 1 - z)

        @pl.when(inside(down))
        def _():
            send_down(down)

        for stage in range(stages - 1, -1, -1):
            now = tick - 2 - depth - stage

            @pl.when(inside(now))
            def _():
                add_replica(stage, now)

        own = tick - 1 - depth

        @pl.when(inside(own))
        def _():
            inner_step(own)

    def tell(owner, target):
        return pltpu.make_async_remote_copy(
            src_ref=squares.at[owner], dst_ref=squares.at[owner],
            send_sem=square_send.at[target], recv_sem=square_recv.at[owner],
            device_id=(rep, target), device_id_type=MESH,
        )

    @pl.loop(1, shards)
    def _(step):
        tell(shard, lax.rem(shard + step, shards)).start()

    @pl.loop(0, chunks)
    def _(k):
        swap(k).wait_send()
        for dest in range(levels):
            @pl.when(dest != z)
            def _():
                hop(k, dest, dest, above).wait_send()

        for stage in range(stages):
            double(stage, k).wait_send()
        load_param(MOMENTUM, k).wait()

    @pl.loop(1, shards)
    def _(step):
        tell(lax.rem(shard + step, shards), lax.rem(shard + step, shards)).wait_recv()

    total = squares[0]
    for owner in range(1, shards):
        total += squares[owner]
    norm = jnp.sqrt(jnp.sum(total, keepdims=True))
    ceiling = 0.3 * math.sqrt(rows * shards * chunks * width)
    factor = ceiling / jnp.maximum(norm, ceiling)

    @pl.loop(0, chunks)
    def _(k):
        here = columns(k)
        scaled = factor * doubled[stages - 1, k]
        momentum = momentum_coef * out_momentum[:, here] + scaled
        out_momentum[:, here] = momentum
        out_anchor[:, here] -= outer_rate * (scaled + momentum_coef * momentum)

    @pl.loop(1, shards)
    def _(step):
        tell(shard, lax.rem(shard + step, shards)).wait_send()


def store(*refs):
    count = len(refs) // 2
    copies = [
        pltpu.make_async_copy(refs[i], refs[count + i], refs[-1].at[i]) for i in range(count)
    ]
    for copy in copies:
        copy.start()
    for copy in copies:
        copy.wait()


def per_device(replicas, shards, *args):
    acts, grads, anchor = args[:3]
    tokens, features = acts.shape[1:]
    rows, width = anchor.shape[0], anchor.shape[1] // CHUNKS
    levels = shards // CORES
    stages = replicas.bit_length() - 1
    f32 = jnp.float32
    dma = pltpu.SemaphoreType.DMA
    scratch = [
        pltpu.VMEM((tokens, features), acts.dtype),
        pltpu.VMEM((features, tokens), acts.dtype),
        pltpu.VMEM((CHUNKS, tokens, width), grads.dtype),
        pltpu.VMEM((CHUNKS, CORES, levels, rows, width), f32),
        pltpu.VMEM((CHUNKS, levels, rows, width), f32),
        pltpu.VMEM((CHUNKS, levels + 1, rows, width), f32),
        pltpu.VMEM((CHUNKS, rows, width), f32),
        pltpu.VMEM((stages, CHUNKS, rows, width), f32),
        pltpu.VMEM((shards, 8, 128), f32),
        dma, dma((CHUNKS,)), dma((5, CHUNKS)),
        dma((CHUNKS,)), dma((CHUNKS,)),
        dma((CHUNKS, levels)), dma((CHUNKS, levels + 1)),
        dma((stages, CHUNKS)), dma((stages, CHUNKS)),
        dma((shards,)), dma((shards,)),
    ]
    shapes = ((1,) + anchor.shape,) * 2 + (anchor.shape,) * 2
    anywhere = pl.BlockSpec(memory_space=pl.ANY)
    results = pl.pallas_call(
        functools.partial(kernel, replicas, shards),
        out_shape=tuple(pltpu.VMEM(shape, f32) for shape in shapes),
        in_specs=[pl.BlockSpec(memory_space=pltpu.HBM)] * 7,
        out_specs=(pl.BlockSpec(memory_space=pltpu.VMEM),) * 4,
        scratch_shapes=scratch,
        compiler_params=pltpu.CompilerParams(
            collective_id=0, has_side_effects=True, vmem_limit_bytes=56 * 2**20
        ),
        cost_estimate=pl.CostEstimate(
            flops=2 * tokens * features * anchor.shape[1],
            bytes_accessed=2 * tokens * anchor.shape[1] + 5 * 4 * anchor.size,
            transcendentals=anchor.size,
        ),
        name="outer_step",
    )(*args)
    return pl.pallas_call(
        store,
        out_shape=tuple(jax.ShapeDtypeStruct(shape, f32) for shape in shapes),
        in_specs=[anywhere] * 4,
        out_specs=(anywhere,) * 4,
        scratch_shapes=[dma((4,))],
        cost_estimate=pl.CostEstimate(
            flops=0, bytes_accessed=4 * 4 * anchor.size, transcendentals=0
        ),
        name="store_results",
    )(*results)


def solution(mesh):
    shared = P("fsdp", None)
    own = P("rep", "fsdp", None)
    return jax.shard_map(
        functools.partial(per_device, mesh.shape["rep"], mesh.shape["fsdp"]),
        mesh=mesh,
        in_specs=(own, own, shared, own, own, own, shared),
        out_specs=(own, own, shared, shared),
        check_vma=False,
    )
```

```python
import functools
import math

import jax
import jax.numpy as jnp
from jax import lax
from jax.experimental import pallas as pl
from jax.experimental.pallas import tpu as pltpu
from jax.sharding import PartitionSpec as P

INNER_STEP = 100
CORES = 2
CHUNKS = 8

beta_first = 0.9
beta_second = 0.95
inner_rate = 0.5
decay_weight = 0.1
outer_rate = 0.7
momentum_coef = 0.9
correction_one = 1.0 - beta_first**INNER_STEP
correction_two = 1.0 - beta_second**INNER_STEP

MESH = pl.DeviceIdType.MESH
ANCHOR, DRIFT, FIRST, SECOND, MOMENTUM = range(5)
AHEAD = 2
SLACK = 2


def kernel(
    replicas, shards,
    acts_hbm, grads_hbm, anchor_hbm, drift_hbm, first_hbm, second_hbm, momentum_hbm,
    out_first, out_second, out_momentum, out_anchor,
    acts, acts_t, grads, part, swapped, chain, pseudo, doubled, squares,
    acts_sem, grads_sem, params_sem,
    swap_send, swap_recv, chain_send, chain_recv, double_send, double_recv,
    square_send, square_recv,
):
    chunks, _, width = grads.shape
    rows = pseudo.shape[1]
    levels = shards // CORES
    stages = doubled.shape[0]
    rep = lax.axis_index("rep")
    shard = lax.axis_index("fsdp")
    z = shard // CORES
    core = shard % CORES
    other = 1 - core
    twin = (rep, z * CORES + other)
    above = (rep, lax.rem(shard + CORES, shards))
    below = (rep, lax.rem(shard + shards - CORES, shards))
    partners = []
    for stage in range(stages):
        bit = 2**stage
        partners.append(rep + bit - 2 * bit * ((rep // bit) % 2))

    barrier = pltpu.get_barrier_semaphore()

    @pl.loop(1, shards)
    def _(step):
        pl.semaphore_signal(
            barrier, inc=1, device_id=(rep, lax.rem(shard + step, shards)), device_id_type=MESH
        )

    for partner in partners:
        pl.semaphore_signal(barrier, inc=1, device_id=(partner, shard), device_id_type=MESH)

    def columns(k):
        return pl.ds(pl.multiple_of(k * width, width), width)

    def load_acts():
        return pltpu.make_async_copy(acts_hbm.at[0], acts, acts_sem)

    def load_grads(k):
        return pltpu.make_async_copy(
            grads_hbm.at[0, :, columns(k)], grads.at[k], grads_sem.at[k]
        )

    def load_param(which, k):
        source, target = (
            (anchor_hbm, out_anchor),
            (drift_hbm.at[0], None),
            (first_hbm.at[0], out_first.at[0]),
            (second_hbm.at[0], out_second.at[0]),
            (momentum_hbm, out_momentum),
        )[which]
        return pltpu.make_async_copy(
            source.at[:, columns(k)],
            pseudo.at[k] if which == DRIFT else target.at[:, columns(k)],
            params_sem.at[which, k],
        )

    load_acts().start()

    for k in range(AHEAD):
        load_grads(k).start()

    load_acts().wait()
    acts_t[...] = acts[...].T
    squares[shard] = jnp.zeros((8, 128), jnp.float32)
    pl.semaphore_wait(barrier, shards - 1 + stages)

    def swap(k):
        return pltpu.make_async_remote_copy(
            src_ref=part.at[k, other], dst_ref=swapped.at[k],
            send_sem=swap_send.at[k], recv_sem=swap_recv.at[k],
            device_id=twin, device_id_type=MESH,
        )

    def hop(k, dest, slot, target):
        return pltpu.make_async_remote_copy(
            src_ref=part.at[k, core, dest], dst_ref=chain.at[k, slot],
            send_sem=chain_send.at[k, dest], recv_sem=chain_recv.at[k, slot],
            device_id=target, device_id_type=MESH,
        )

    def double(stage, k):
        turn = lax.rem(k + stage, stages)
        partner = partners[0]
        for j in range(1, stages):
            partner = jnp.where(turn == j, partners[j], partner)
        source = pseudo.at[k] if stage == 0 else doubled.at[stage - 1, k]
        return pltpu.make_async_remote_copy(
            src_ref=source, dst_ref=doubled.at[stage, k],
            send_sem=double_send.at[stage, k], recv_sem=double_recv.at[stage, k],
            device_id=(partner, shard), device_id_type=MESH,
        )

    def inside(k):
        return (k >= 0) & (k < chunks)

    def product(k):
        load_grads(k).wait()

        @pl.when(k + AHEAD < chunks)
        def _():
            load_grads(k + AHEAD).start()

        for which in range(5):
            load_param(which, k).start()

        for at in range(0, width, 256):
            block = jnp.dot(
                acts_t[...], grads[k, :, at : at + 256], preferred_element_type=jnp.float32
            )
            for j in range(shards):
                part[k, j % CORES, j // CORES, :, at : at + 256] = block[j * rows : (j + 1) * rows]
        swap(k).start()

    def join(k):
        swap(k).wait_recv()
        part[k, core] += swapped[k]

    def add_hop(k, dest):
        hop(k, dest, dest, above).wait_recv()
        part[k, core, dest] += chain[k, dest]

    def send_up(k):
        for dest in range(levels - 1, 0, -1):
            @pl.when(dest > z)
            def _():
                @pl.when(z > 0)
                def _():
                    add_hop(k, dest)

                hop(k, dest, dest, above).start()

    def send_down(k):
        for dest in range(levels - 1):
            @pl.when(dest < z)
            def _():
                @pl.when(z < levels - 1)
                def _():
                    add_hop(k, dest)

                hop(k, dest, jnp.where(dest == z - 1, levels, dest), below).start()

    def inner_step(k):
        @pl.when(z > 0)
        def _():
            hop(k, z, z, above).wait_recv()
            part[k, core, z] += chain[k, z]

        @pl.when(z < levels - 1)
        def _():
            hop(k, z, levels, above).wait_recv()
            part[k, core, z] += chain[k, levels]

        for which in range(4):
            load_param(which, k).wait()
        here = columns(k)
        gradient = part[k, core, z]
        drift = pseudo[k]
        moment_one = beta_first * out_first[0, :, here] + (1.0 - beta_first) * gradient
        moment_two = beta_second * out_second[0, :, here] + (1.0 - beta_second) * gradient * gradient
        update = moment_one / correction_one / (
            jnp.sqrt(moment_two / correction_two) + 1e-08
        ) + decay_weight * (out_anchor[:, here] + drift)
        pseudo[k] = inner_rate * update - drift
        double(0, k).start()
        out_first[0, :, here] = moment_one
        out_second[0, :, here] = moment_two

    def add_replica(stage, k):
        double(stage, k).wait_recv()
        mine = pseudo[k] if stage == 0 else doubled[stage - 1, k]
        total = mine + doubled[stage, k]
        if stage < stages - 1:
            doubled[stage, k] = total
            double(stage + 1, k).start()
        else:
            average = total / replicas
            doubled[stage, k] = average
            square = average * average
            folded = jnp.zeros((8, 128), jnp.float32)
            for i in range(0, rows, 8):
                for j in range(0, width, 128):
                    folded += square[i : i + 8, j : j + 128]
            squares[shard] += folded

    depth = SLACK * jnp.maximum(z, levels - 1 - z)

    @pl.loop(0, chunks + 1 + SLACK * (levels - 1 + stages))
    def _(tick):
        @pl.when(inside(tick))
        def _():
            product(tick)

        @pl.when(inside(tick - 1))
        def _():
            join(tick - 1)

        up = tick - 1 - SLACK * z

        @pl.when(inside(up))
        def _():
            send_up(up)

        down = tick - 1 - SLACK * (levels - 1 - z)

        @pl.when(inside(down))
        def _():
            send_down(down)

        for stage in range(stages - 1, -1, -1):
            now = tick - 1 - depth - SLACK * (stage + 1)

            @pl.when(inside(now))
            def _():
                add_replica(stage, now)

        own = tick - 1 - depth

        @pl.when(inside(own))
        def _():
            inner_step(own)

    def tell(owner, target):
        return pltpu.make_async_remote_copy(
            src_ref=squares.at[owner], dst_ref=squares.at[owner],
            send_sem=square_send.at[target], recv_sem=square_recv.at[owner],
            device_id=(rep, target), device_id_type=MESH,
        )

    @pl.loop(1, shards)
    def _(step):
        tell(shard, lax.rem(shard + step, shards)).start()

    @pl.loop(0, chunks)
    def _(k):
        swap(k).wait_send()
        for dest in range(levels):
            @pl.when(dest != z)
            def _():
                hop(k, dest, dest, above).wait_send()

        for stage in range(stages):
            double(stage, k).wait_send()
        load_param(MOMENTUM, k).wait()

    @pl.loop(1, shards)
    def _(step):
        tell(lax.rem(shard + step, shards), lax.rem(shard + step, shards)).wait_recv()

    total = squares[0]
    for owner in range(1, shards):
        total += squares[owner]
    norm = jnp.sqrt(jnp.sum(total, keepdims=True))
    ceiling = 0.3 * math.sqrt(rows * shards * chunks * width)
    factor = ceiling / jnp.maximum(norm, ceiling)

    @pl.loop(0, chunks)
    def _(k):
        here = columns(k)
        scaled = factor * doubled[stages - 1, k]
        momentum = momentum_coef * out_momentum[:, here] + scaled
        out_momentum[:, here] = momentum
        out_anchor[:, here] -= outer_rate * (scaled + momentum_coef * momentum)

    @pl.loop(1, shards)
    def _(step):
        tell(shard, lax.rem(shard + step, shards)).wait_send()


def store(*refs):
    count = len(refs) // 2
    copies = [
        pltpu.make_async_copy(refs[i], refs[count + i], refs[-1].at[i]) for i in range(count)
    ]
    for copy in copies:
        copy.start()
    for copy in copies:
        copy.wait()


def per_device(replicas, shards, *args):
    acts, grads, anchor = args[:3]
    tokens, features = acts.shape[1:]
    rows, width = anchor.shape[0], anchor.shape[1] // CHUNKS
    levels = shards // CORES
    stages = replicas.bit_length() - 1
    f32 = jnp.float32
    dma = pltpu.SemaphoreType.DMA
    scratch = [
        pltpu.VMEM((tokens, features), acts.dtype),
        pltpu.VMEM((features, tokens), acts.dtype),
        pltpu.VMEM((CHUNKS, tokens, width), grads.dtype),
        pltpu.VMEM((CHUNKS, CORES, levels, rows, width), f32),
        pltpu.VMEM((CHUNKS, levels, rows, width), f32),
        pltpu.VMEM((CHUNKS, levels + 1, rows, width), f32),
        pltpu.VMEM((CHUNKS, rows, width), f32),
        pltpu.VMEM((stages, CHUNKS, rows, width), f32),
        pltpu.VMEM((shards, 8, 128), f32),
        dma, dma((CHUNKS,)), dma((5, CHUNKS)),
        dma((CHUNKS,)), dma((CHUNKS,)),
        dma((CHUNKS, levels)), dma((CHUNKS, levels + 1)),
        dma((stages, CHUNKS)), dma((stages, CHUNKS)),
        dma((shards,)), dma((shards,)),
    ]
    shapes = ((1,) + anchor.shape,) * 2 + (anchor.shape,) * 2
    anywhere = pl.BlockSpec(memory_space=pl.ANY)
    results = pl.pallas_call(
        functools.partial(kernel, replicas, shards),
        out_shape=tuple(pltpu.VMEM(shape, f32) for shape in shapes),
        in_specs=[pl.BlockSpec(memory_space=pltpu.HBM)] * 7,
        out_specs=(pl.BlockSpec(memory_space=pltpu.VMEM),) * 4,
        scratch_shapes=scratch,
        compiler_params=pltpu.CompilerParams(
            collective_id=0, has_side_effects=True, vmem_limit_bytes=56 * 2**20
        ),
        cost_estimate=pl.CostEstimate(
            flops=2 * tokens * features * anchor.shape[1],
            bytes_accessed=2 * tokens * anchor.shape[1] + 5 * 4 * anchor.size,
            transcendentals=anchor.size,
        ),
        name="outer_step",
    )(*args)
    return pl.pallas_call(
        store,
        out_shape=tuple(jax.ShapeDtypeStruct(shape, f32) for shape in shapes),
        in_specs=[pl.BlockSpec(memory_space=pltpu.VMEM)] * 4,
        out_specs=(anywhere,) * 4,
        scratch_shapes=[dma((4,))],
        cost_estimate=pl.CostEstimate(
            flops=0, bytes_accessed=4 * 4 * anchor.size, transcendentals=0
        ),
        name="store_results",
    )(*results)


def solution(mesh):
    shared = P("fsdp", None)
    own = P("rep", "fsdp", None)
    return jax.shard_map(
        functools.partial(per_device, mesh.shape["rep"], mesh.shape["fsdp"]),
        mesh=mesh,
        in_specs=(own, own, shared, own, own, own, shared),
        out_specs=(own, own, shared, shared),
        check_vma=False,
    )
```

```python
import functools
import math

import jax
import jax.numpy as jnp
from jax import lax
from jax.experimental import pallas as pl
from jax.experimental.pallas import tpu as pltpu
from jax.sharding import PartitionSpec as P

INNER_STEP = 100
CORES = 2
CHUNKS = 16

beta_first = 0.9
beta_second = 0.95
inner_rate = 0.5
decay_weight = 0.1
outer_rate = 0.7
momentum_coef = 0.9
correction_one = 1.0 - beta_first**INNER_STEP
correction_two = 1.0 - beta_second**INNER_STEP

MESH = pl.DeviceIdType.MESH
ANCHOR, DRIFT, FIRST, SECOND, MOMENTUM = range(5)
AHEAD = 4
SLACK = 2


def kernel(
    replicas, shards,
    acts_hbm, grads_hbm, anchor_hbm, drift_hbm, first_hbm, second_hbm, momentum_hbm,
    out_first, out_second, out_momentum, out_anchor,
    acts, acts_t, grads, part, swapped, chain, pseudo, doubled, squares,
    acts_sem, grads_sem, params_sem,
    swap_send, swap_recv, chain_send, chain_recv, double_send, double_recv,
    square_send, square_recv,
):
    chunks, _, width = grads.shape
    rows = pseudo.shape[1]
    levels = shards // CORES
    stages = doubled.shape[0]
    rep = lax.axis_index("rep")
    shard = lax.axis_index("fsdp")
    z = shard // CORES
    core = shard % CORES
    other = 1 - core
    twin = (rep, z * CORES + other)
    above = (rep, lax.rem(shard + CORES, shards))
    below = (rep, lax.rem(shard + shards - CORES, shards))
    opposite = (rep, (levels - 1 - z) * CORES + core)
    partners = []
    for stage in range(stages):
        bit = 2**stage
        partners.append(rep + bit - 2 * bit * ((rep // bit) % 2))

    barrier = pltpu.get_barrier_semaphore()

    @pl.loop(1, shards)
    def _(step):
        pl.semaphore_signal(
            barrier, inc=1, device_id=(rep, lax.rem(shard + step, shards)), device_id_type=MESH
        )

    for partner in partners:
        pl.semaphore_signal(barrier, inc=1, device_id=(partner, shard), device_id_type=MESH)

    def columns(k):
        return pl.ds(pl.multiple_of(k * width, width), width)

    def load_acts():
        return pltpu.make_async_copy(acts_hbm.at[0], acts, acts_sem)

    def load_grads(k):
        return pltpu.make_async_copy(
            grads_hbm.at[0, :, columns(k)], grads.at[k], grads_sem.at[k]
        )

    def load_param(which, k):
        source, target = (
            (anchor_hbm, out_anchor),
            (drift_hbm.at[0], None),
            (first_hbm.at[0], out_first.at[0]),
            (second_hbm.at[0], out_second.at[0]),
            (momentum_hbm, out_momentum),
        )[which]
        return pltpu.make_async_copy(
            source.at[:, columns(k)],
            pseudo.at[k] if which == DRIFT else target.at[:, columns(k)],
            params_sem.at[which, k],
        )

    load_acts().start()

    for k in range(AHEAD):
        load_grads(k).start()

    load_acts().wait()
    acts_t[...] = acts[...].T
    squares[shard] = jnp.zeros((8, 128), jnp.float32)
    pl.semaphore_wait(barrier, shards - 1 + stages)

    def swap(k):
        return pltpu.make_async_remote_copy(
            src_ref=part.at[k, other], dst_ref=swapped.at[k],
            send_sem=swap_send.at[k], recv_sem=swap_recv.at[k],
            device_id=twin, device_id_type=MESH,
        )

    def hop(k, dest, slot, target):
        return pltpu.make_async_remote_copy(
            src_ref=part.at[k, core, dest], dst_ref=chain.at[k, slot],
            send_sem=chain_send.at[k, dest], recv_sem=chain_recv.at[k, slot],
            device_id=target, device_id_type=MESH,
        )

    def double(stage, k):
        turn = lax.rem(k + stage, stages)
        partner = partners[0]
        for j in range(1, stages):
            partner = jnp.where(turn == j, partners[j], partner)
        source = pseudo.at[k] if stage == 0 else doubled.at[stage - 1, k]
        return pltpu.make_async_remote_copy(
            src_ref=source, dst_ref=doubled.at[stage, k],
            send_sem=double_send.at[stage, k], recv_sem=double_recv.at[stage, k],
            device_id=(partner, shard), device_id_type=MESH,
        )

    def inside(k):
        return (k >= 0) & (k < chunks)

    def product(k):
        load_grads(k).wait()

        @pl.when(k + AHEAD < chunks)
        def _():
            load_grads(k + AHEAD).start()

        for which in range(5):
            load_param(which, k).start()

        for at in range(0, width, 256):
            block = jnp.dot(
                acts_t[...], grads[k, :, at : at + 256], preferred_element_type=jnp.float32
            )
            for j in range(shards):
                part[k, j % CORES, j // CORES, :, at : at + 256] = block[j * rows : (j + 1) * rows]
        swap(k).start()

    def join(k):
        swap(k).wait_recv()
        part[k, core] += swapped[k]

    def add_hop(k, dest):
        hop(k, dest, dest, above).wait_recv()
        part[k, core, dest] += chain[k, dest]

    def send_up(k):
        for dest in range(levels - 1, 0, -1):
            first = 1 if dest == levels - 1 else 0

            @pl.when((dest > z) & (z >= first))
            def _():
                @pl.when(z > first)
                def _():
                    add_hop(k, dest)

                hop(k, dest, dest, above).start()

        @pl.when(z == 0)
        def _():
            hop(k, levels - 1, levels + 1, opposite).start()

    def send_down(k):
        for dest in range(levels - 1):
            first = levels - 2 if dest == 0 else levels - 1

            @pl.when((dest < z) & (z <= first))
            def _():
                @pl.when(z < first)
                def _():
                    add_hop(k, dest)

                hop(k, dest, jnp.where(dest == z - 1, levels, dest), below).start()

        @pl.when(z == levels - 1)
        def _():
            hop(k, 0, levels + 1, opposite).start()

    def inner_step(k):
        @pl.when(z > 0)
        def _():
            hop(k, z, z, above).wait_recv()
            part[k, core, z] += chain[k, z]

        @pl.when(z < levels - 1)
        def _():
            hop(k, z, levels, above).wait_recv()
            part[k, core, z] += chain[k, levels]

        @pl.when((z == 0) | (z == levels - 1))
        def _():
            hop(k, z, levels + 1, opposite).wait_recv()
            part[k, core, z] += chain[k, levels + 1]

        for which in range(4):
            load_param(which, k).wait()
        here = columns(k)
        gradient = part[k, core, z]
        drift = pseudo[k]
        moment_one = beta_first * out_first[0, :, here] + (1.0 - beta_first) * gradient
        moment_two = beta_second * out_second[0, :, here] + (1.0 - beta_second) * gradient * gradient
        update = moment_one / correction_one / (
            jnp.sqrt(moment_two / correction_two) + 1e-08
        ) + decay_weight * (out_anchor[:, here] + drift)
        pseudo[k] = inner_rate * update - drift
        double(0, k).start()
        out_first[0, :, here] = moment_one
        out_second[0, :, here] = moment_two

    def add_replica(stage, k):
        double(stage, k).wait_recv()
        mine = pseudo[k] if stage == 0 else doubled[stage - 1, k]
        total = mine + doubled[stage, k]
        if stage < stages - 1:
            doubled[stage, k] = total
            double(stage + 1, k).start()
        else:
            average = total / replicas
            doubled[stage, k] = average
            square = average * average
            folded = jnp.zeros((8, 128), jnp.float32)
            for i in range(0, rows, 8):
                for j in range(0, width, 128):
                    folded += square[i : i + 8, j : j + 128]
            squares[shard] += folded

    depth = SLACK * jnp.maximum(z, levels - 1 - z)

    @pl.loop(0, chunks + 1 + SLACK * (levels - 1 + stages))
    def _(tick):
        @pl.when(inside(tick))
        def _():
            product(tick)

        @pl.when(inside(tick - 1))
        def _():
            join(tick - 1)

        up = tick - 1 - SLACK * z

        @pl.when(inside(up))
        def _():
            send_up(up)

        down = tick - 1 - SLACK * (levels - 1 - z)

        @pl.when(inside(down))
        def _():
            send_down(down)

        for stage in range(stages - 1, -1, -1):
            now = tick - 1 - depth - SLACK * (stage + 1)

            @pl.when(inside(now))
            def _():
                add_replica(stage, now)

        own = tick - 1 - depth

        @pl.when(inside(own))
        def _():
            inner_step(own)

    def tell(owner, target):
        return pltpu.make_async_remote_copy(
            src_ref=squares.at[owner], dst_ref=squares.at[owner],
            send_sem=square_send.at[target], recv_sem=square_recv.at[owner],
            device_id=(rep, target), device_id_type=MESH,
        )

    @pl.loop(1, shards)
    def _(step):
        tell(shard, lax.rem(shard + step, shards)).start()

    @pl.loop(0, chunks)
    def _(k):
        swap(k).wait_send()
        for dest in range(levels):
            @pl.when(dest != z)
            def _():
                hop(k, dest, dest, above).wait_send()

        for stage in range(stages):
            double(stage, k).wait_send()
        load_param(MOMENTUM, k).wait()

    @pl.loop(1, shards)
    def _(step):
        tell(lax.rem(shard + step, shards), lax.rem(shard + step, shards)).wait_recv()

    total = squares[0]
    for owner in range(1, shards):
        total += squares[owner]
    norm = jnp.sqrt(jnp.sum(total, keepdims=True))
    ceiling = 0.3 * math.sqrt(rows * shards * chunks * width)
    factor = ceiling / jnp.maximum(norm, ceiling)

    @pl.loop(0, chunks)
    def _(k):
        here = columns(k)
        scaled = factor * doubled[stages - 1, k]
        momentum = momentum_coef * out_momentum[:, here] + scaled
        out_momentum[:, here] = momentum
        out_anchor[:, here] -= outer_rate * (scaled + momentum_coef * momentum)

    @pl.loop(1, shards)
    def _(step):
        tell(shard, lax.rem(shard + step, shards)).wait_send()


def per_device(replicas, shards, *args):
    acts, grads, anchor = args[:3]
    tokens, features = acts.shape[1:]
    rows, width = anchor.shape[0], anchor.shape[1] // CHUNKS
    levels = shards // CORES
    stages = replicas.bit_length() - 1
    f32 = jnp.float32
    dma = pltpu.SemaphoreType.DMA
    scratch = [
        pltpu.VMEM((tokens, features), acts.dtype),
        pltpu.VMEM((features, tokens), acts.dtype),
        pltpu.VMEM((CHUNKS, tokens, width), grads.dtype),
        pltpu.VMEM((CHUNKS, CORES, levels, rows, width), f32),
        pltpu.VMEM((CHUNKS, levels, rows, width), f32),
        pltpu.VMEM((CHUNKS, levels + 2, rows, width), f32),
        pltpu.VMEM((CHUNKS, rows, width), f32),
        pltpu.VMEM((stages, CHUNKS, rows, width), f32),
        pltpu.VMEM((shards, 8, 128), f32),
        dma, dma((CHUNKS,)), dma((5, CHUNKS)),
        dma((CHUNKS,)), dma((CHUNKS,)),
        dma((CHUNKS, levels)), dma((CHUNKS, levels + 2)),
        dma((stages, CHUNKS)), dma((stages, CHUNKS)),
        dma((shards,)), dma((shards,)),
    ]
    shapes = ((1,) + anchor.shape,) * 2 + (anchor.shape,) * 2
    return pl.pallas_call(
        functools.partial(kernel, replicas, shards),
        out_shape=tuple(pltpu.VMEM(shape, f32) for shape in shapes),
        in_specs=[pl.BlockSpec(memory_space=pltpu.HBM)] * 7,
        out_specs=(pl.BlockSpec(memory_space=pltpu.VMEM),) * 4,
        scratch_shapes=scratch,
        compiler_params=pltpu.CompilerParams(
            collective_id=0, has_side_effects=True, vmem_limit_bytes=56 * 2**20
        ),
        cost_estimate=pl.CostEstimate(
            flops=2 * tokens * features * anchor.shape[1],
            bytes_accessed=2 * tokens * anchor.shape[1] + 5 * 4 * anchor.size,
            transcendentals=anchor.size,
        ),
        name="outer_step",
    )(*args)

def solution(mesh):
    shared = P("fsdp", None)
    own = P("rep", "fsdp", None)
    return jax.shard_map(
        functools.partial(per_device, mesh.shape["rep"], mesh.shape["fsdp"]),
        mesh=mesh,
        in_specs=(own, own, shared, own, own, own, shared),
        out_specs=(own, own, shared, shared),
        check_vma=False,
    )
```

```python
import functools
import math

import jax
import jax.numpy as jnp
from jax import lax
from jax.experimental import pallas as pl
from jax.experimental.pallas import tpu as pltpu
from jax.sharding import PartitionSpec as P

INNER_STEP = 100
CORES = 2
CHUNKS = 16

beta_first = 0.9
beta_second = 0.95
inner_rate = 0.5
decay_weight = 0.1
outer_rate = 0.7
momentum_coef = 0.9
correction_one = 1.0 - beta_first**INNER_STEP
correction_two = 1.0 - beta_second**INNER_STEP

MESH = pl.DeviceIdType.MESH
ANCHOR, DRIFT, FIRST, SECOND, MOMENTUM = range(5)
AHEAD = 4
SLACK = 2
HALVES = 2


def kernel(
    replicas, shards,
    acts_hbm, grads_hbm, anchor_hbm, drift_hbm, first_hbm, second_hbm, momentum_hbm,
    out_first, out_second, out_momentum, out_anchor,
    acts, acts_t, grads, part, swapped, chain, pseudo, doubled, squares,
    acts_sem, grads_sem, params_sem,
    swap_send, swap_recv, chain_send, chain_recv, double_send, double_recv,
    square_send, square_recv,
):
    chunks, _, width = grads.shape
    rows = pseudo.shape[1]
    levels = shards // CORES
    stages = doubled.shape[0]
    rep = lax.axis_index("rep")
    shard = lax.axis_index("fsdp")
    z = shard // CORES
    core = shard % CORES
    other = 1 - core
    twin = (rep, z * CORES + other)
    above = (rep, lax.rem(shard + CORES, shards))
    below = (rep, lax.rem(shard + shards - CORES, shards))
    opposite = (rep, (levels - 1 - z) * CORES + core)
    partners = []
    for stage in range(stages):
        bit = 2**stage
        partners.append(rep + bit - 2 * bit * ((rep // bit) % 2))

    barrier = pltpu.get_barrier_semaphore()

    @pl.loop(1, shards)
    def _(step):
        pl.semaphore_signal(
            barrier, inc=1, device_id=(rep, lax.rem(shard + step, shards)), device_id_type=MESH
        )

    for partner in partners:
        pl.semaphore_signal(barrier, inc=1, device_id=(partner, shard), device_id_type=MESH)

    def columns(k):
        return pl.ds(pl.multiple_of(k * width, width), width)

    def load_acts():
        return pltpu.make_async_copy(acts_hbm.at[0], acts, acts_sem)

    def load_grads(k):
        return pltpu.make_async_copy(
            grads_hbm.at[0, :, columns(k)], grads.at[k], grads_sem.at[k]
        )

    def load_param(which, k):
        source, target = (
            (anchor_hbm, out_anchor),
            (drift_hbm.at[0], None),
            (first_hbm.at[0], out_first.at[0]),
            (second_hbm.at[0], out_second.at[0]),
            (momentum_hbm, out_momentum),
        )[which]
        return pltpu.make_async_copy(
            source.at[:, columns(k)],
            pseudo.at[k] if which == DRIFT else target.at[:, columns(k)],
            params_sem.at[which, k],
        )

    load_acts().start()

    for k in range(AHEAD):
        load_grads(k).start()

    load_acts().wait()
    acts_t[...] = acts[...].T
    squares[shard] = jnp.zeros((8, 128), jnp.float32)
    pl.semaphore_wait(barrier, shards - 1 + stages)

    def swap(k):
        return pltpu.make_async_remote_copy(
            src_ref=part.at[k, other], dst_ref=swapped.at[k],
            send_sem=swap_send.at[k], recv_sem=swap_recv.at[k],
            device_id=twin, device_id_type=MESH,
        )

    def hop(k, dest, slot, target):
        return pltpu.make_async_remote_copy(
            src_ref=part.at[k, core, dest], dst_ref=chain.at[k, slot],
            send_sem=chain_send.at[k, dest], recv_sem=chain_recv.at[k, slot],
            device_id=target, device_id_type=MESH,
        )

    def double(stage, k, half):
        partner = partners[(stage + half) % stages]
        size = rows // HALVES
        some = pl.ds(half * size, size)
        source = pseudo if stage == 0 else doubled.at[stage - 1]
        return pltpu.make_async_remote_copy(
            src_ref=source.at[k, some], dst_ref=doubled.at[stage, k, some],
            send_sem=double_send.at[stage, k, half], recv_sem=double_recv.at[stage, k, half],
            device_id=(partner, shard), device_id_type=MESH,
        )

    def inside(k):
        return (k >= 0) & (k < chunks)

    def product(k):
        load_grads(k).wait()

        @pl.when(k + AHEAD < chunks)
        def _():
            load_grads(k + AHEAD).start()

        for which in range(5):
            load_param(which, k).start()

        for at in range(0, width, 256):
            block = jnp.dot(
                acts_t[...], grads[k, :, at : at + 256], preferred_element_type=jnp.float32
            )
            for j in range(shards):
                part[k, j % CORES, j // CORES, :, at : at + 256] = block[j * rows : (j + 1) * rows]
        swap(k).start()

    def join(k):
        swap(k).wait_recv()
        part[k, core] += swapped[k]

    def add_hop(k, dest):
        hop(k, dest, dest, above).wait_recv()
        part[k, core, dest] += chain[k, dest]

    def send_up(k):
        for dest in range(levels - 1, 0, -1):
            first = 1 if dest == levels - 1 else 0

            @pl.when((dest > z) & (z >= first))
            def _():
                @pl.when(z > first)
                def _():
                    add_hop(k, dest)

                hop(k, dest, dest, above).start()

        @pl.when(z == 0)
        def _():
            hop(k, levels - 1, levels + 1, opposite).start()

    def send_down(k):
        for dest in range(levels - 1):
            first = levels - 2 if dest == 0 else levels - 1

            @pl.when((dest < z) & (z <= first))
            def _():
                @pl.when(z < first)
                def _():
                    add_hop(k, dest)

                hop(k, dest, jnp.where(dest == z - 1, levels, dest), below).start()

        @pl.when(z == levels - 1)
        def _():
            hop(k, 0, levels + 1, opposite).start()

    def inner_step(k):
        @pl.when(z > 0)
        def _():
            hop(k, z, z, above).wait_recv()
            part[k, core, z] += chain[k, z]

        @pl.when(z < levels - 1)
        def _():
            hop(k, z, levels, above).wait_recv()
            part[k, core, z] += chain[k, levels]

        @pl.when((z == 0) | (z == levels - 1))
        def _():
            hop(k, z, levels + 1, opposite).wait_recv()
            part[k, core, z] += chain[k, levels + 1]

        for which in range(4):
            load_param(which, k).wait()
        here = columns(k)
        gradient = part[k, core, z]
        drift = pseudo[k]
        moment_one = beta_first * out_first[0, :, here] + (1.0 - beta_first) * gradient
        moment_two = beta_second * out_second[0, :, here] + (1.0 - beta_second) * gradient * gradient
        update = moment_one / correction_one / (
            jnp.sqrt(moment_two / correction_two) + 1e-08
        ) + decay_weight * (out_anchor[:, here] + drift)
        pseudo[k] = inner_rate * update - drift
        for half in range(HALVES):
            double(0, k, half).start()
        out_first[0, :, here] = moment_one
        out_second[0, :, here] = moment_two

    def add_replica(stage, k):
        for half in range(HALVES):
            double(stage, k, half).wait_recv()
        mine = pseudo[k] if stage == 0 else doubled[stage - 1, k]
        total = mine + doubled[stage, k]
        if stage < stages - 1:
            doubled[stage, k] = total
            for half in range(HALVES):
                double(stage + 1, k, half).start()
        else:
            average = total / replicas
            doubled[stage, k] = average
            square = average * average
            folded = jnp.zeros((8, 128), jnp.float32)
            for i in range(0, rows, 8):
                for j in range(0, width, 128):
                    folded += square[i : i + 8, j : j + 128]
            squares[shard] += folded

    def settle(k):
        swap(k).wait_send()
        for dest in range(levels):
            @pl.when(dest != z)
            def _():
                hop(k, dest, dest, above).wait_send()

        for stage in range(stages):
            for half in range(HALVES):
                double(stage, k, half).wait_send()
        load_param(MOMENTUM, k).wait()

    depth = SLACK * jnp.maximum(z, levels - 1 - z)

    @pl.loop(0, chunks + 1 + SLACK * (levels - 1 + stages))
    def _(tick):
        @pl.when(inside(tick))
        def _():
            product(tick)

        @pl.when(inside(tick - 1))
        def _():
            join(tick - 1)

        up = tick - 1 - SLACK * z

        @pl.when(inside(up))
        def _():
            send_up(up)

        down = tick - 1 - SLACK * (levels - 1 - z)

        @pl.when(inside(down))
        def _():
            send_down(down)

        for stage in range(stages - 1, -1, -1):
            now = tick - 1 - depth - SLACK * (stage + 1)

            @pl.when(inside(now))
            def _():
                add_replica(stage, now)

        old = tick - 2 - depth - SLACK * stages

        @pl.when((old >= 0) & (old < chunks - 1))
        def _():
            settle(old)

        own = tick - 1 - depth

        @pl.when(inside(own))
        def _():
            inner_step(own)

    def tell(owner, target):
        return pltpu.make_async_remote_copy(
            src_ref=squares.at[owner], dst_ref=squares.at[owner],
            send_sem=square_send.at[target], recv_sem=square_recv.at[owner],
            device_id=(rep, target), device_id_type=MESH,
        )

    @pl.loop(1, shards)
    def _(step):
        tell(shard, lax.rem(shard + step, shards)).start()

    settle(chunks - 1)

    @pl.loop(1, shards)
    def _(step):
        tell(lax.rem(shard + step, shards), lax.rem(shard + step, shards)).wait_recv()

    total = squares[0]
    for owner in range(1, shards):
        total += squares[owner]
    norm = jnp.sqrt(jnp.sum(total, keepdims=True))
    ceiling = 0.3 * math.sqrt(rows * shards * chunks * width)
    factor = ceiling / jnp.maximum(norm, ceiling)

    @pl.loop(0, chunks)
    def _(k):
        here = columns(k)
        scaled = factor * doubled[stages - 1, k]
        momentum = momentum_coef * out_momentum[:, here] + scaled
        out_momentum[:, here] = momentum
        out_anchor[:, here] -= outer_rate * (scaled + momentum_coef * momentum)

    @pl.loop(1, shards)
    def _(step):
        tell(shard, lax.rem(shard + step, shards)).wait_send()


def per_device(replicas, shards, *args):
    acts, grads, anchor = args[:3]
    tokens, features = acts.shape[1:]
    rows, width = anchor.shape[0], anchor.shape[1] // CHUNKS
    levels = shards // CORES
    stages = replicas.bit_length() - 1
    f32 = jnp.float32
    dma = pltpu.SemaphoreType.DMA
    scratch = [
        pltpu.VMEM((tokens, features), acts.dtype),
        pltpu.VMEM((features, tokens), acts.dtype),
        pltpu.VMEM((CHUNKS, tokens, width), grads.dtype),
        pltpu.VMEM((CHUNKS, CORES, levels, rows, width), f32),
        pltpu.VMEM((CHUNKS, levels, rows, width), f32),
        pltpu.VMEM((CHUNKS, levels + 2, rows, width), f32),
        pltpu.VMEM((CHUNKS, rows, width), f32),
        pltpu.VMEM((stages, CHUNKS, rows, width), f32),
        pltpu.VMEM((shards, 8, 128), f32),
        dma, dma((CHUNKS,)), dma((5, CHUNKS)),
        dma((CHUNKS,)), dma((CHUNKS,)),
        dma((CHUNKS, levels)), dma((CHUNKS, levels + 2)),
        dma((stages, CHUNKS, HALVES)), dma((stages, CHUNKS, HALVES)),
        dma((shards,)), dma((shards,)),
    ]
    shapes = ((1,) + anchor.shape,) * 2 + (anchor.shape,) * 2
    return pl.pallas_call(
        functools.partial(kernel, replicas, shards),
        out_shape=tuple(pltpu.VMEM(shape, f32) for shape in shapes),
        in_specs=[pl.BlockSpec(memory_space=pltpu.HBM)] * 7,
        out_specs=(pl.BlockSpec(memory_space=pltpu.VMEM),) * 4,
        scratch_shapes=scratch,
        compiler_params=pltpu.CompilerParams(
            collective_id=0, has_side_effects=True, vmem_limit_bytes=56 * 2**20
        ),
        cost_estimate=pl.CostEstimate(
            flops=2 * tokens * features * anchor.shape[1],
            bytes_accessed=2 * tokens * anchor.shape[1] + 5 * 4 * anchor.size,
            transcendentals=anchor.size,
        ),
        name="outer_step",
    )(*args)

def solution(mesh):
    shared = P("fsdp", None)
    own = P("rep", "fsdp", None)
    return jax.shard_map(
        functools.partial(per_device, mesh.shape["rep"], mesh.shape["fsdp"]),
        mesh=mesh,
        in_specs=(own, own, shared, own, own, own, shared),
        out_specs=(own, own, shared, shared),
        check_vma=False,
    )
```

```python
import functools
import math

import jax
import jax.numpy as jnp
from jax import lax
from jax.experimental import pallas as pl
from jax.experimental.pallas import tpu as pltpu
from jax.sharding import PartitionSpec as P

INNER_STEP = 100
CORES = 2
CHUNKS = 8

beta_first = 0.9
beta_second = 0.95
inner_rate = 0.5
decay_weight = 0.1
outer_rate = 0.7
momentum_coef = 0.9
correction_one = 1.0 - beta_first**INNER_STEP
correction_two = 1.0 - beta_second**INNER_STEP

MESH = pl.DeviceIdType.MESH
ANCHOR, DRIFT, FIRST, SECOND, MOMENTUM = range(5)
AHEAD = 2
SLACK = 2
HALVES = 2


def kernel(
    replicas, shards,
    acts_hbm, grads_hbm, anchor_hbm, drift_hbm, first_hbm, second_hbm, momentum_hbm,
    out_first, out_second, out_momentum, out_anchor,
    acts, acts_t, grads, part, swapped, chain, pseudo, doubled, squares,
    acts_sem, grads_sem, params_sem,
    swap_send, swap_recv, chain_send, chain_recv, double_send, double_recv,
    square_send, square_recv,
):
    chunks, _, width = grads.shape
    rows = pseudo.shape[1]
    levels = shards // CORES
    stages = doubled.shape[0]
    rep = lax.axis_index("rep")
    shard = lax.axis_index("fsdp")
    z = shard // CORES
    core = shard % CORES
    other = 1 - core
    twin = (rep, z * CORES + other)
    above = (rep, lax.rem(shard + CORES, shards))
    below = (rep, lax.rem(shard + shards - CORES, shards))
    opposite = (rep, (levels - 1 - z) * CORES + core)
    partners = []
    for stage in range(stages):
        bit = 2**stage
        partners.append(rep + bit - 2 * bit * ((rep // bit) % 2))

    barrier = pltpu.get_barrier_semaphore()

    @pl.loop(1, shards)
    def _(step):
        pl.semaphore_signal(
            barrier, inc=1, device_id=(rep, lax.rem(shard + step, shards)), device_id_type=MESH
        )

    for partner in partners:
        pl.semaphore_signal(barrier, inc=1, device_id=(partner, shard), device_id_type=MESH)

    def columns(k):
        return pl.ds(pl.multiple_of(k * width, width), width)

    def load_acts():
        return pltpu.make_async_copy(acts_hbm.at[0], acts, acts_sem)

    def load_grads(k):
        return pltpu.make_async_copy(
            grads_hbm.at[0, :, columns(k)], grads.at[k], grads_sem.at[k]
        )

    def load_param(which, k):
        source, target = (
            (anchor_hbm, out_anchor),
            (drift_hbm.at[0], None),
            (first_hbm.at[0], out_first.at[0]),
            (second_hbm.at[0], out_second.at[0]),
            (momentum_hbm, out_momentum),
        )[which]
        return pltpu.make_async_copy(
            source.at[:, columns(k)],
            pseudo.at[k] if which == DRIFT else target.at[:, columns(k)],
            params_sem.at[which, k],
        )

    load_acts().start()

    for k in range(AHEAD):
        load_grads(k).start()

    load_acts().wait()
    acts_t[...] = acts[...].T
    squares[shard] = jnp.zeros((8, 128), jnp.float32)
    pl.semaphore_wait(barrier, shards - 1 + stages)

    def swap(k):
        return pltpu.make_async_remote_copy(
            src_ref=part.at[k, other], dst_ref=swapped.at[k],
            send_sem=swap_send.at[k], recv_sem=swap_recv.at[k],
            device_id=twin, device_id_type=MESH,
        )

    def hop(k, dest, slot, target):
        return pltpu.make_async_remote_copy(
            src_ref=part.at[k, core, dest], dst_ref=chain.at[k, slot],
            send_sem=chain_send.at[k, dest], recv_sem=chain_recv.at[k, slot],
            device_id=target, device_id_type=MESH,
        )

    def double(stage, k, half):
        partner = partners[(stage + half) % stages]
        size = rows // HALVES
        some = pl.ds(half * size, size)
        source = pseudo if stage == 0 else doubled.at[stage - 1]
        return pltpu.make_async_remote_copy(
            src_ref=source.at[k, some], dst_ref=doubled.at[stage, k, some],
            send_sem=double_send.at[stage, k, half], recv_sem=double_recv.at[stage, k, half],
            device_id=(partner, shard), device_id_type=MESH,
        )

    def inside(k):
        return (k >= 0) & (k < chunks)

    def product(k):
        load_grads(k).wait()

        @pl.when(k + AHEAD < chunks)
        def _():
            load_grads(k + AHEAD).start()

        for which in range(5):
            load_param(which, k).start()

        for at in range(0, width, 256):
            block = jnp.dot(
                acts_t[...], grads[k, :, at : at + 256], preferred_element_type=jnp.float32
            )
            for j in range(shards):
                part[k, j % CORES, j // CORES, :, at : at + 256] = block[j * rows : (j + 1) * rows]
        swap(k).start()

    def join(k):
        swap(k).wait_recv()
        part[k, core] += swapped[k]

    def add_hop(k, dest):
        hop(k, dest, dest, above).wait_recv()
        part[k, core, dest] += chain[k, dest]

    def send_up(k):
        for dest in range(levels - 1, 0, -1):
            first = 1 if dest == levels - 1 else 0

            @pl.when((dest > z) & (z >= first))
            def _():
                @pl.when(z > first)
                def _():
                    add_hop(k, dest)

                hop(k, dest, dest, above).start()

        @pl.when(z == 0)
        def _():
            hop(k, levels - 1, levels + 1, opposite).start()

    def send_down(k):
        for dest in range(levels - 1):
            first = levels - 2 if dest == 0 else levels - 1

            @pl.when((dest < z) & (z <= first))
            def _():
                @pl.when(z < first)
                def _():
                    add_hop(k, dest)

                hop(k, dest, jnp.where(dest == z - 1, levels, dest), below).start()

        @pl.when(z == levels - 1)
        def _():
            hop(k, 0, levels + 1, opposite).start()

    def inner_step(k):
        @pl.when(z > 0)
        def _():
            hop(k, z, z, above).wait_recv()
            part[k, core, z] += chain[k, z]

        @pl.when(z < levels - 1)
        def _():
            hop(k, z, levels, above).wait_recv()
            part[k, core, z] += chain[k, levels]

        @pl.when((z == 0) | (z == levels - 1))
        def _():
            hop(k, z, levels + 1, opposite).wait_recv()
            part[k, core, z] += chain[k, levels + 1]

        for which in range(4):
            load_param(which, k).wait()
        here = columns(k)
        gradient = part[k, core, z]
        drift = pseudo[k]
        moment_one = beta_first * out_first[0, :, here] + (1.0 - beta_first) * gradient
        moment_two = beta_second * out_second[0, :, here] + (1.0 - beta_second) * gradient * gradient
        update = moment_one / correction_one / (
            jnp.sqrt(moment_two / correction_two) + 1e-08
        ) + decay_weight * (out_anchor[:, here] + drift)
        pseudo[k] = inner_rate * update - drift
        for half in range(HALVES):
            double(0, k, half).start()
        out_first[0, :, here] = moment_one
        out_second[0, :, here] = moment_two

    def add_replica(stage, k):
        for half in range(HALVES):
            double(stage, k, half).wait_recv()
        mine = pseudo[k] if stage == 0 else doubled[stage - 1, k]
        total = mine + doubled[stage, k]
        if stage < stages - 1:
            doubled[stage, k] = total
            for half in range(HALVES):
                double(stage + 1, k, half).start()
        else:
            average = total / replicas
            doubled[stage, k] = average
            square = average * average
            folded = jnp.zeros((8, 128), jnp.float32)
            for i in range(0, rows, 8):
                for j in range(0, width, 128):
                    folded += square[i : i + 8, j : j + 128]
            squares[shard] += folded

    def settle(k):
        swap(k).wait_send()
        for dest in range(levels):
            @pl.when(dest != z)
            def _():
                hop(k, dest, dest, above).wait_send()

        for stage in range(stages):
            for half in range(HALVES):
                double(stage, k, half).wait_send()
        load_param(MOMENTUM, k).wait()

    depth = SLACK * jnp.maximum(z, levels - 1 - z)

    @pl.loop(0, chunks + 1 + SLACK * (levels - 1 + stages))
    def _(tick):
        @pl.when(inside(tick))
        def _():
            product(tick)

        @pl.when(inside(tick - 1))
        def _():
            join(tick - 1)

        up = tick - 1 - SLACK * z

        @pl.when(inside(up))
        def _():
            send_up(up)

        down = tick - 1 - SLACK * (levels - 1 - z)

        @pl.when(inside(down))
        def _():
            send_down(down)

        for stage in range(stages - 1, -1, -1):
            now = tick - 1 - depth - SLACK * (stage + 1)

            @pl.when(inside(now))
            def _():
                add_replica(stage, now)

        old = tick - 2 - depth - SLACK * stages

        @pl.when((old >= 0) & (old < chunks - 1))
        def _():
            settle(old)

        own = tick - 1 - depth

        @pl.when(inside(own))
        def _():
            inner_step(own)

    def tell(owner, target):
        return pltpu.make_async_remote_copy(
            src_ref=squares.at[owner], dst_ref=squares.at[owner],
            send_sem=square_send.at[target], recv_sem=square_recv.at[owner],
            device_id=(rep, target), device_id_type=MESH,
        )

    @pl.loop(1, shards)
    def _(step):
        tell(shard, lax.rem(shard + step, shards)).start()

    settle(chunks - 1)

    @pl.loop(1, shards)
    def _(step):
        tell(lax.rem(shard + step, shards), lax.rem(shard + step, shards)).wait_recv()

    total = squares[0]
    for owner in range(1, shards):
        total += squares[owner]
    norm = jnp.sqrt(jnp.sum(total, keepdims=True))
    ceiling = 0.3 * math.sqrt(rows * shards * chunks * width)
    factor = ceiling / jnp.maximum(norm, ceiling)

    @pl.loop(0, chunks)
    def _(k):
        here = columns(k)
        scaled = factor * doubled[stages - 1, k]
        momentum = momentum_coef * out_momentum[:, here] + scaled
        out_momentum[:, here] = momentum
        out_anchor[:, here] -= outer_rate * (scaled + momentum_coef * momentum)

    @pl.loop(1, shards)
    def _(step):
        tell(shard, lax.rem(shard + step, shards)).wait_send()


def per_device(replicas, shards, *args):
    acts, grads, anchor = args[:3]
    tokens, features = acts.shape[1:]
    rows, width = anchor.shape[0], anchor.shape[1] // CHUNKS
    levels = shards // CORES
    stages = replicas.bit_length() - 1
    f32 = jnp.float32
    dma = pltpu.SemaphoreType.DMA
    scratch = [
        pltpu.VMEM((tokens, features), acts.dtype),
        pltpu.VMEM((features, tokens), acts.dtype),
        pltpu.VMEM((CHUNKS, tokens, width), grads.dtype),
        pltpu.VMEM((CHUNKS, CORES, levels, rows, width), f32),
        pltpu.VMEM((CHUNKS, levels, rows, width), f32),
        pltpu.VMEM((CHUNKS, levels + 2, rows, width), f32),
        pltpu.VMEM((CHUNKS, rows, width), f32),
        pltpu.VMEM((stages, CHUNKS, rows, width), f32),
        pltpu.VMEM((shards, 8, 128), f32),
        dma, dma((CHUNKS,)), dma((5, CHUNKS)),
        dma((CHUNKS,)), dma((CHUNKS,)),
        dma((CHUNKS, levels)), dma((CHUNKS, levels + 2)),
        dma((stages, CHUNKS, HALVES)), dma((stages, CHUNKS, HALVES)),
        dma((shards,)), dma((shards,)),
    ]
    shapes = ((1,) + anchor.shape,) * 2 + (anchor.shape,) * 2
    return pl.pallas_call(
        functools.partial(kernel, replicas, shards),
        out_shape=tuple(pltpu.VMEM(shape, f32) for shape in shapes),
        in_specs=[pl.BlockSpec(memory_space=pltpu.HBM)] * 7,
        out_specs=(pl.BlockSpec(memory_space=pltpu.VMEM),) * 4,
        scratch_shapes=scratch,
        compiler_params=pltpu.CompilerParams(
            collective_id=0, has_side_effects=True, vmem_limit_bytes=56 * 2**20
        ),
        cost_estimate=pl.CostEstimate(
            flops=2 * tokens * features * anchor.shape[1],
            bytes_accessed=2 * tokens * anchor.shape[1] + 5 * 4 * anchor.size,
            transcendentals=anchor.size,
        ),
        name="outer_step",
    )(*args)

def solution(mesh):
    shared = P("fsdp", None)
    own = P("rep", "fsdp", None)
    return jax.shard_map(
        functools.partial(per_device, mesh.shape["rep"], mesh.shape["fsdp"]),
        mesh=mesh,
        in_specs=(own, own, shared, own, own, own, shared),
        out_specs=(own, own, shared, shared),
        check_vma=False,
    )
```

```python
import functools
import math

import jax
import jax.numpy as jnp
from jax import lax
from jax.experimental import pallas as pl
from jax.experimental.pallas import tpu as pltpu
from jax.sharding import PartitionSpec as P

INNER_STEP = 100
CORES = 2
CHUNKS = 32

beta_first = 0.9
beta_second = 0.95
inner_rate = 0.5
decay_weight = 0.1
outer_rate = 0.7
momentum_coef = 0.9
correction_one = 1.0 - beta_first**INNER_STEP
correction_two = 1.0 - beta_second**INNER_STEP

MESH = pl.DeviceIdType.MESH
ANCHOR, DRIFT, FIRST, SECOND, MOMENTUM = range(5)
AHEAD = 8
SLACK = 2
HALVES = 2


def kernel(
    replicas, shards,
    acts_hbm, grads_hbm, anchor_hbm, drift_hbm, first_hbm, second_hbm, momentum_hbm,
    out_first, out_second, out_momentum, out_anchor,
    acts, acts_t, grads, part, swapped, chain, pseudo, doubled, squares,
    acts_sem, grads_sem, params_sem,
    swap_send, swap_recv, chain_send, chain_recv, double_send, double_recv,
    square_send, square_recv,
):
    chunks, _, width = grads.shape
    rows = pseudo.shape[1]
    levels = shards // CORES
    stages = doubled.shape[0]
    rep = lax.axis_index("rep")
    shard = lax.axis_index("fsdp")
    z = shard // CORES
    core = shard % CORES
    other = 1 - core
    twin = (rep, z * CORES + other)
    above = (rep, lax.rem(shard + CORES, shards))
    below = (rep, lax.rem(shard + shards - CORES, shards))
    opposite = (rep, (levels - 1 - z) * CORES + core)
    partners = []
    for stage in range(stages):
        bit = 2**stage
        partners.append(rep + bit - 2 * bit * ((rep // bit) % 2))

    barrier = pltpu.get_barrier_semaphore()

    @pl.loop(1, shards)
    def _(step):
        pl.semaphore_signal(
            barrier, inc=1, device_id=(rep, lax.rem(shard + step, shards)), device_id_type=MESH
        )

    for partner in partners:
        pl.semaphore_signal(barrier, inc=1, device_id=(partner, shard), device_id_type=MESH)

    def columns(k):
        return pl.ds(pl.multiple_of(k * width, width), width)

    def load_acts():
        return pltpu.make_async_copy(acts_hbm.at[0], acts, acts_sem)

    def load_grads(k):
        return pltpu.make_async_copy(
            grads_hbm.at[0, :, columns(k)], grads.at[k], grads_sem.at[k]
        )

    def load_param(which, k):
        source, target = (
            (anchor_hbm, out_anchor),
            (drift_hbm.at[0], None),
            (first_hbm.at[0], out_first.at[0]),
            (second_hbm.at[0], out_second.at[0]),
            (momentum_hbm, out_momentum),
        )[which]
        return pltpu.make_async_copy(
            source.at[:, columns(k)],
            pseudo.at[k] if which == DRIFT else target.at[:, columns(k)],
            params_sem.at[which, k],
        )

    load_acts().start()

    for k in range(AHEAD):
        load_grads(k).start()

    load_acts().wait()
    acts_t[...] = acts[...].T
    squares[shard] = jnp.zeros((8, 128), jnp.float32)
    pl.semaphore_wait(barrier, shards - 1 + stages)

    def swap(k):
        return pltpu.make_async_remote_copy(
            src_ref=part.at[k, other], dst_ref=swapped.at[k],
            send_sem=swap_send.at[k], recv_sem=swap_recv.at[k],
            device_id=twin, device_id_type=MESH,
        )

    def hop(k, dest, slot, target):
        return pltpu.make_async_remote_copy(
            src_ref=part.at[k, core, dest], dst_ref=chain.at[k, slot],
            send_sem=chain_send.at[k, dest], recv_sem=chain_recv.at[k, slot],
            device_id=target, device_id_type=MESH,
        )

    def double(stage, k, half):
        partner = partners[(stage + half) % stages]
        size = rows // HALVES
        some = pl.ds(half * size, size)
        source = pseudo if stage == 0 else doubled.at[stage - 1]
        return pltpu.make_async_remote_copy(
            src_ref=source.at[k, some], dst_ref=doubled.at[stage, k, some],
            send_sem=double_send.at[stage, k, half], recv_sem=double_recv.at[stage, k, half],
            device_id=(partner, shard), device_id_type=MESH,
        )

    def inside(k):
        return (k >= 0) & (k < chunks)

    def product(k):
        load_grads(k).wait()

        @pl.when(k + AHEAD < chunks)
        def _():
            load_grads(k + AHEAD).start()

        for which in range(5):
            load_param(which, k).start()

        for at in range(0, width, 256):
            block = jnp.dot(
                acts_t[...], grads[k, :, at : at + 256], preferred_element_type=jnp.float32
            )
            for j in range(shards):
                part[k, j % CORES, j // CORES, :, at : at + 256] = block[j * rows : (j + 1) * rows]
        swap(k).start()

    def join(k):
        swap(k).wait_recv()
        part[k, core] += swapped[k]

    def add_hop(k, dest):
        hop(k, dest, dest, above).wait_recv()
        part[k, core, dest] += chain[k, dest]

    def send_up(k):
        for dest in range(levels - 1, 0, -1):
            first = 1 if dest == levels - 1 else 0

            @pl.when((dest > z) & (z >= first))
            def _():
                @pl.when(z > first)
                def _():
                    add_hop(k, dest)

                hop(k, dest, dest, above).start()

        @pl.when(z == 0)
        def _():
            hop(k, levels - 1, levels + 1, opposite).start()

    def send_down(k):
        for dest in range(levels - 1):
            first = levels - 2 if dest == 0 else levels - 1

            @pl.when((dest < z) & (z <= first))
            def _():
                @pl.when(z < first)
                def _():
                    add_hop(k, dest)

                hop(k, dest, jnp.where(dest == z - 1, levels, dest), below).start()

        @pl.when(z == levels - 1)
        def _():
            hop(k, 0, levels + 1, opposite).start()

    def inner_step(k):
        @pl.when(z > 0)
        def _():
            hop(k, z, z, above).wait_recv()
            part[k, core, z] += chain[k, z]

        @pl.when(z < levels - 1)
        def _():
            hop(k, z, levels, above).wait_recv()
            part[k, core, z] += chain[k, levels]

        @pl.when((z == 0) | (z == levels - 1))
        def _():
            hop(k, z, levels + 1, opposite).wait_recv()
            part[k, core, z] += chain[k, levels + 1]

        for which in range(4):
            load_param(which, k).wait()
        here = columns(k)
        gradient = part[k, core, z]
        drift = pseudo[k]
        moment_one = beta_first * out_first[0, :, here] + (1.0 - beta_first) * gradient
        moment_two = beta_second * out_second[0, :, here] + (1.0 - beta_second) * gradient * gradient
        update = moment_one / correction_one / (
            jnp.sqrt(moment_two / correction_two) + 1e-08
        ) + decay_weight * (out_anchor[:, here] + drift)
        pseudo[k] = inner_rate * update - drift
        for half in range(HALVES):
            double(0, k, half).start()
        out_first[0, :, here] = moment_one
        out_second[0, :, here] = moment_two

    def add_replica(stage, k):
        for half in range(HALVES):
            double(stage, k, half).wait_recv()
        mine = pseudo[k] if stage == 0 else doubled[stage - 1, k]
        total = mine + doubled[stage, k]
        if stage < stages - 1:
            doubled[stage, k] = total
            for half in range(HALVES):
                double(stage + 1, k, half).start()
        else:
            average = total / replicas
            doubled[stage, k] = average
            square = average * average
            folded = jnp.zeros((8, 128), jnp.float32)
            for i in range(0, rows, 8):
                for j in range(0, width, 128):
                    folded += square[i : i + 8, j : j + 128]
            squares[shard] += folded

    def settle(k):
        swap(k).wait_send()
        for dest in range(levels):
            @pl.when(dest != z)
            def _():
                hop(k, dest, dest, above).wait_send()

        for stage in range(stages):
            for half in range(HALVES):
                double(stage, k, half).wait_send()
        load_param(MOMENTUM, k).wait()

    depth = SLACK * jnp.maximum(z, levels - 1 - z)

    @pl.loop(0, chunks + 1 + SLACK * (levels - 1 + stages))
    def _(tick):
        @pl.when(inside(tick))
        def _():
            product(tick)

        @pl.when(inside(tick - 1))
        def _():
            join(tick - 1)

        up = tick - 1 - SLACK * z

        @pl.when(inside(up))
        def _():
            send_up(up)

        down = tick - 1 - SLACK * (levels - 1 - z)

        @pl.when(inside(down))
        def _():
            send_down(down)

        for stage in range(stages - 1, -1, -1):
            now = tick - 1 - depth - SLACK * (stage + 1)

            @pl.when(inside(now))
            def _():
                add_replica(stage, now)

        old = tick - 2 - depth - SLACK * stages

        @pl.when((old >= 0) & (old < chunks - 1))
        def _():
            settle(old)

        own = tick - 1 - depth

        @pl.when(inside(own))
        def _():
            inner_step(own)

    def tell(owner, target):
        return pltpu.make_async_remote_copy(
            src_ref=squares.at[owner], dst_ref=squares.at[owner],
            send_sem=square_send.at[target], recv_sem=square_recv.at[owner],
            device_id=(rep, target), device_id_type=MESH,
        )

    @pl.loop(1, shards)
    def _(step):
        tell(shard, lax.rem(shard + step, shards)).start()

    settle(chunks - 1)

    @pl.loop(1, shards)
    def _(step):
        tell(lax.rem(shard + step, shards), lax.rem(shard + step, shards)).wait_recv()

    total = squares[0]
    for owner in range(1, shards):
        total += squares[owner]
    norm = jnp.sqrt(jnp.sum(total, keepdims=True))
    ceiling = 0.3 * math.sqrt(rows * shards * chunks * width)
    factor = ceiling / jnp.maximum(norm, ceiling)

    @pl.loop(0, chunks)
    def _(k):
        here = columns(k)
        scaled = factor * doubled[stages - 1, k]
        momentum = momentum_coef * out_momentum[:, here] + scaled
        out_momentum[:, here] = momentum
        out_anchor[:, here] -= outer_rate * (scaled + momentum_coef * momentum)

    @pl.loop(1, shards)
    def _(step):
        tell(shard, lax.rem(shard + step, shards)).wait_send()


def per_device(replicas, shards, *args):
    acts, grads, anchor = args[:3]
    tokens, features = acts.shape[1:]
    rows, width = anchor.shape[0], anchor.shape[1] // CHUNKS
    levels = shards // CORES
    stages = replicas.bit_length() - 1
    f32 = jnp.float32
    dma = pltpu.SemaphoreType.DMA
    scratch = [
        pltpu.VMEM((tokens, features), acts.dtype),
        pltpu.VMEM((features, tokens), acts.dtype),
        pltpu.VMEM((CHUNKS, tokens, width), grads.dtype),
        pltpu.VMEM((CHUNKS, CORES, levels, rows, width), f32),
        pltpu.VMEM((CHUNKS, levels, rows, width), f32),
        pltpu.VMEM((CHUNKS, levels + 2, rows, width), f32),
        pltpu.VMEM((CHUNKS, rows, width), f32),
        pltpu.VMEM((stages, CHUNKS, rows, width), f32),
        pltpu.VMEM((shards, 8, 128), f32),
        dma, dma((CHUNKS,)), dma((5, CHUNKS)),
        dma((CHUNKS,)), dma((CHUNKS,)),
        dma((CHUNKS, levels)), dma((CHUNKS, levels + 2)),
        dma((stages, CHUNKS, HALVES)), dma((stages, CHUNKS, HALVES)),
        dma((shards,)), dma((shards,)),
    ]
    shapes = ((1,) + anchor.shape,) * 2 + (anchor.shape,) * 2
    return pl.pallas_call(
        functools.partial(kernel, replicas, shards),
        out_shape=tuple(pltpu.VMEM(shape, f32) for shape in shapes),
        in_specs=[pl.BlockSpec(memory_space=pltpu.HBM)] * 7,
        out_specs=(pl.BlockSpec(memory_space=pltpu.VMEM),) * 4,
        scratch_shapes=scratch,
        compiler_params=pltpu.CompilerParams(
            collective_id=0, has_side_effects=True, vmem_limit_bytes=56 * 2**20
        ),
        cost_estimate=pl.CostEstimate(
            flops=2 * tokens * features * anchor.shape[1],
            bytes_accessed=2 * tokens * anchor.shape[1] + 5 * 4 * anchor.size,
            transcendentals=anchor.size,
        ),
        name="outer_step",
    )(*args)

def solution(mesh):
    shared = P("fsdp", None)
    own = P("rep", "fsdp", None)
    return jax.shard_map(
        functools.partial(per_device, mesh.shape["rep"], mesh.shape["fsdp"]),
        mesh=mesh,
        in_specs=(own, own, shared, own, own, own, shared),
        out_specs=(own, own, shared, shared),
        check_vma=False,
    )
```
